32 devices in a mesh: pipe: 4 (over z), tensor: 4 (over y, core), dp: 2 (over x).
Axes of the slice: x: 2, y: 2, z: 4, core: 2. Of those that a mesh axis runs over, the one named last changes fastest.
Arguments:
- query_heads: bfloat16 [8, 512, 4096], P(('dp', 'pipe'), None, 'tensor'), parts along dimension 0, may hold values from -5 to 5, as said below
- key_heads: bfloat16 [8, 512, 4096], P(('dp', 'pipe'), None, 'tensor'), parts along dimension 0, may hold values from -5 to 5
- value_heads: bfloat16 [8, 512, 4096], P(('dp', 'pipe'), None, 'tensor'), parts along dimension 0, may hold values from -16 to 16
- segment_ids: int32 [8, 512], P(('dp', 'pipe')), parts along dimension 0, may hold values from 0 to 3, never falling along the last dimension, each value on 1 to 256 neighbouring positions
- section_input: bfloat16 [8, 512, 8192], P(('dp', 'pipe'), 'tensor'), parts along dimension 0, may hold values from -6 to 6
- out_weight: bfloat16 [8, 4096, 8192], P(('dp', 'pipe'), 'tensor'), parts along dimension 0, may hold values from -0.1875 to 0.1875
Outputs:
- received: bfloat16 [8, 512, 8192], P(('dp', 'pipe'), 'tensor'), parts along dimension 0
- evicted: bfloat16 [8, 512, 8192], P(('dp', 'pipe'), 'tensor'), parts along dimension 0
- evicted_scale: float32 [8, 512], P(('dp', 'pipe'), 'tensor'), parts along dimension 0
The draws below stay inside these ranges and needn't reach their ends.
There are 2 independent parts, one for each index of `dp`. The reference program is written for one: setup_inputs(seed, part) draws one part's arguments, and reference() takes and returns one part's arrays. A program takes and returns all parts, laid end to end along the dimension named above; each array names one. Nothing has to cross between parts.
Inputs may be any that keep to these rules, and one draw needn't show every extreme that they name: `query_heads`: queries and keys are bfloat16 values of moderate size. `segment_ids`: each section's segment numbers never fall along the tokens; every document is 1 to 256 tokens long.
All inputs are finite; a program needn't handle non-finite values. Where the reference program divides by a largest or mean magnitude, that divisor is 1e-20 or more.
Results may differ from the reference program's by a relative error of at most 0.0055.
Values may be sent and summed in bfloat16 or wider, within the bound.
No kernel may reach another device: no remote copies, remote signals or barrier semaphores. Data moves between devices by JAX's collectives and lax.ppermute only.
A program may use at most 128 MiB of HBM per device.

```python
import math
import jax
import jax.numpy as jnp
import numpy as np
from jax import lax

D = 8192
HEADS = 32
HD = 128
ROWS = 512
SECTIONS = 4


def shared_draw(key):
    base_key = jax.random.fold_in(key, 7311)
    query_key, key_key = jax.random.split(base_key, 2)
    shape = (SECTIONS, ROWS, HEADS * HD)
    query_base = jnp.clip(jax.random.normal(query_key, shape, jnp.float32), -4.0, 4.0)
    key_base = jnp.clip(jax.random.normal(key_key, shape, jnp.float32), -4.0, 4.0)
    return (query_base, key_base)


def draw_query_heads(key, part):
    return shared_draw(key)[0].astype(jnp.bfloat16)


def draw_key_heads(key, part):
    return shared_draw(key)[1].astype(jnp.bfloat16)


def level_of(own_key, shape, cuts, low, high):
    def one(dim, blocks):
        draws = jax.random.uniform(jax.random.fold_in(jax.random.fold_in(own_key, 6), dim), (blocks,), jnp.float32, low / len(cuts), high / len(cuts))
        return jnp.repeat(jnp.exp(draws), shape[dim] // blocks).reshape((-1,) + (1,) * (len(shape) - dim - 1))

    level = one(*cuts[0])
    for cut in cuts[1:]:
        level = level * one(*cut)
    return level


def split_up(amount, total, most, skew):
    loads = [(1 << 20) // math.isqrt(rank ** skew) + 1 for rank in range(2, amount + 1)]
    spare, counts = total - most - (amount - 1), [1] * (amount - 1)
    while spare > 0:
        candidates = [i for i in range(amount - 1) if counts[i] < most]
        mass, budget = sum([loads[i] for i in candidates]), spare
        for i in candidates:
            addition = min(most - counts[i], max(1, budget * loads[i] // mass), spare)
            counts[i] = counts[i] + addition
            spare = spare - addition
    return np.array([most] + counts)


def uneven_parts(stream_key, count, total, limit, lean):
    if count == 2:
        one = jax.random.randint(stream_key, (), max(1, total - limit), min(limit, total - 1) + 1)
        return jnp.stack([one, total - one])
    sizes = jnp.asarray(split_up(count, total, limit, lean), jnp.int32)
    pairs = (count - 1) // 2
    donor, sink = sizes[1:1 + 2 * pairs:2], sizes[2:2 + 2 * pairs:2]
    margin = jnp.minimum(donor - 1, limit - sink)
    moved = jax.random.randint(jax.random.fold_in(stream_key, 1), (pairs,), 0, 1 << 20) % (margin + 1)
    sizes = sizes.at[1:1 + 2 * pairs:2].set(donor - moved).at[2:2 + 2 * pairs:2].set(sink + moved)
    return sizes[jax.random.permutation(jax.random.fold_in(stream_key, 2), count)]


def centred(own_key, dims, width, most, cuts=(), kind=jnp.bfloat16):
    loudness = level_of(own_key, dims, cuts, -0.22, 0.18) if cuts else 1.0
    result = jax.random.normal(own_key, dims, jnp.float32) * width * loudness
    return jnp.minimum(jnp.maximum(result, -most), most).astype(kind)


def setup_inputs(seed: int = 0, part: int = 0) -> dict:
    seeds = jax.random.split(jax.random.key(seed), 7)
    own_keys = jax.random.split(jax.random.fold_in(seeds[6], part), 7)
    query_heads = draw_query_heads(jax.random.fold_in(jax.random.fold_in(seeds[6], part), 71), part)
    key_heads = draw_key_heads(jax.random.fold_in(jax.random.fold_in(seeds[6], part), 71), part)
    value_heads = centred(own_keys[2], (SECTIONS, ROWS, HEADS * HD), 4.0, 16.0, ((0, 4), (2, 4)))
    segment_ids = jax.vmap(lambda own: jnp.searchsorted(jnp.cumsum(uneven_parts(own, 4, ROWS, ROWS // 2, 1)), jnp.arange(ROWS), side="right"))(jax.random.split(own_keys[3], SECTIONS)).reshape((SECTIONS, ROWS)).astype(jnp.int32)
    section_input = centred(own_keys[4], (SECTIONS, ROWS, D), 1.0, 6.0, ((0, 4), (1, 4)))
    out_weight = centred(own_keys[5], (SECTIONS, HEADS * HD, D), (HEADS * HD // 4) ** -0.5, 0.1875, ((0, 4), (1, 4)))
    return {"query_heads": query_heads, "key_heads": key_heads, "value_heads": value_heads, "segment_ids": segment_ids, "section_input": section_input, "out_weight": out_weight}


def one_section(operands):
    query_block, key_block, value_block, segment_row, input_block, weight_block = operands
    row_count = query_block.shape[0]
    query_three = query_block.astype(jnp.float32).reshape(row_count, HEADS, HD)
    key_three = key_block.astype(jnp.float32).reshape(row_count, HEADS, HD)
    value_three = value_block.astype(jnp.float32).reshape(row_count, HEADS, HD)
    position = jnp.arange(row_count, dtype=jnp.int32)
    allowed = (segment_row[:, None] == segment_row[None, :]) & (position[None, :] <= position[:, None])
    scores = jnp.einsum('qhd,khd->hqk', query_three, key_three) * (1.0 / math.sqrt(HD))
    scores = jnp.where(allowed[None, :, :], scores, jnp.float32(-1e+30))
    row_max = lax.optimization_barrier(jnp.max(scores, axis=2, keepdims=True))
    expons = jnp.exp(scores - row_max)
    weights = (expons / lax.optimization_barrier(jnp.sum(expons, axis=2, keepdims=True))).astype(jnp.bfloat16)
    heads_out = jnp.einsum('hqk,khd->qhd', weights.astype(jnp.float32), value_three)
    heads_out = heads_out.astype(jnp.bfloat16).reshape(row_count, HEADS * HD)
    partial_value = jnp.dot(heads_out, weight_block, preferred_element_type=jnp.float32)
    section_out = (input_block.astype(jnp.float32) + partial_value).astype(jnp.bfloat16)
    wide_input = input_block.astype(jnp.float32)
    scale = lax.optimization_barrier(jnp.max(jnp.abs(wide_input), axis=1)) + 1e-06
    packed = (wide_input / scale[:, None]).astype(jnp.bfloat16)
    return (section_out, packed, scale)

def reference(query_heads, key_heads, value_heads, segment_ids, section_input, out_weight):
    section_out, packed, scale = lax.map(one_section, (query_heads, key_heads, value_heads, segment_ids, section_input, out_weight))
    received = jnp.concatenate([jnp.zeros_like(section_out[:1]), section_out[:-1]], axis=0)
    evicted = packed[::-1]
    evicted_scale = scale[::-1]
    return (received, evicted, evicted_scale)
```

```python
import math

import jax
import jax.numpy as jnp
from jax import lax
from jax.sharding import PartitionSpec as P

HD = 128
CHUNKS = 4


def attention(query_block, key_block, value_block, segment_row):
    row_count = query_block.shape[0]
    head_count = query_block.shape[1] // HD
    query_three = query_block.reshape(row_count, head_count, HD)
    key_three = key_block.reshape(row_count, head_count, HD)
    value_three = value_block.reshape(row_count, head_count, HD)
    position = jnp.arange(row_count, dtype=jnp.int32)
    allowed = (segment_row[:, None] == segment_row[None, :]) & (
        position[None, :] <= position[:, None]
    )
    scores = jnp.einsum(
        "qhd,khd->hqk", query_three, key_three, preferred_element_type=jnp.float32
    ) * (1.0 / math.sqrt(HD))
    scores = jnp.where(allowed[None, :, :], scores, jnp.float32(-1e30))
    row_max = jnp.max(scores, axis=2, keepdims=True)
    expons = jnp.exp(scores - row_max)
    weights = (expons / jnp.sum(expons, axis=2, keepdims=True)).astype(jnp.bfloat16)
    heads_out = jnp.einsum("hqk,khd->qhd", weights, value_three, preferred_element_type=jnp.float32)
    return heads_out.astype(jnp.bfloat16).reshape(row_count, head_count * HD)


def scattered_sum(heads_out, weight, axis):
    count = lax.axis_size(axis)
    bits = count.bit_length() - 1
    index = lax.axis_index(axis)
    rows, depth = heads_out.shape
    owned = heads_out.reshape((2,) * bits + (rows // count, depth))
    low = index & 1
    theirs = lax.dynamic_index_in_dim(owned, 1 - low, axis=bits - 1, keepdims=False)
    mine = lax.dynamic_index_in_dim(owned, low, axis=bits - 1, keepdims=False)
    dot = lambda part: jnp.dot(
        part.reshape(-1, depth), weight, preferred_element_type=jnp.float32
    ).reshape(part.shape[:-1] + (weight.shape[1],))
    swap = lambda value, bit: lax.ppermute(
        value, axis, [(source, source ^ (1 << bit)) for source in range(count)]
    )
    arrived = swap(dot(theirs).astype(jnp.bfloat16), 0)
    total = dot(mine)
    for bit in range(1, bits):
        mine_bit = (index >> bit) & 1
        pick = lambda value, which: lax.dynamic_index_in_dim(
            value, which, axis=bits - 1 - bit, keepdims=False
        )
        out = pick(total, 1 - mine_bit) + pick(arrived, 1 - mine_bit).astype(jnp.float32)
        total = pick(total, mine_bit) + pick(arrived, mine_bit).astype(jnp.float32)
        arrived = swap(out.astype(jnp.bfloat16), bit)
    return total + arrived.astype(jnp.float32)


def per_device(query_heads, key_heads, value_heads, segment_ids, section_input, out_weight):
    sections = lax.axis_size("pipe")
    mirrored = lax.ppermute(
        section_input, "pipe", [(source, sections - 1 - source) for source in range(sections)]
    )
    heads_out = attention(query_heads[0], key_heads[0], value_heads[0], segment_ids[0])
    width = out_weight.shape[2] // CHUNKS
    pieces = []
    for chunk in range(CHUNKS):
        columns = slice(chunk * width, (chunk + 1) * width)
        mine = scattered_sum(heads_out, out_weight[0, :, columns], "tensor")
        pieces.append((section_input[0, :, columns].astype(jnp.float32) + mine).astype(jnp.bfloat16))
    section_out = jnp.concatenate(pieces, axis=1)
    received = lax.ppermute(
        section_out[None], "pipe", [(source, source + 1) for source in range(sections - 1)]
    )
    wide = mirrored.astype(jnp.float32)
    scale = jnp.max(jnp.abs(wide), axis=2) + 1e-06
    evicted = (wide / scale[:, :, None]).astype(jnp.bfloat16)
    return (received, evicted, scale)


def solution(mesh):
    return jax.shard_map(
        per_device,
        mesh=mesh,
        in_specs=(
            P(("dp", "pipe"), None, "tensor"),
            P(("dp", "pipe"), None, "tensor"),
            P(("dp", "pipe"), None, "tensor"),
            P(("dp", "pipe"), None),
            P(("dp", "pipe"), "tensor", None),
            P(("dp", "pipe"), "tensor", None),
        ),
        out_specs=(
            P(("dp", "pipe"), "tensor", None),
            P(("dp", "pipe"), "tensor", None),
            P(("dp", "pipe"), "tensor"),
        ),
        check_vma=False,
    )
```

```python
import functools
import math

import jax
import jax.numpy as jnp
from jax import lax
from jax.experimental import pallas as pl
from jax.experimental.pallas import tpu as pltpu
from jax.sharding import PartitionSpec as P

HD = 128
CHUNKS = 4
TILE = 512
COST = pl.CostEstimate(flops=1000000, bytes_accessed=100000, transcendentals=0)
LATE = 40000000000


def attention_kernel(query_ref, key_ref, value_ref, row_ref, column_ref, out_ref):
    rows = query_ref.shape[0]
    half = rows // 2 if rows % 256 == 0 else rows
    for begin in range(0, rows, half):
        end = begin + half
        scores = lax.dot_general(
            query_ref[begin:end, :],
            key_ref[:end, :],
            (((1,), (1,)), ((), ())),
            preferred_element_type=jnp.float32,
        ) * (1.0 / math.sqrt(HD))
        query_at = lax.broadcasted_iota(jnp.int32, scores.shape, 0) + begin
        key_at = lax.broadcasted_iota(jnp.int32, scores.shape, 1)
        allowed = (column_ref[begin:end, :] == row_ref[:, :end]) & (key_at <= query_at)
        scores = jnp.where(allowed, scores, jnp.float32(-1e30))
        expons = jnp.exp(scores - jnp.max(scores, axis=1, keepdims=True))
        weights = expons * (1.0 / jnp.sum(expons, axis=1, keepdims=True))
        out_ref[begin:end, :] = jnp.dot(
            weights.astype(jnp.bfloat16), value_ref[:end, :], preferred_element_type=jnp.float32
        ).astype(jnp.bfloat16)


def attention(query, key, value, segment_ids):
    rows, width = query.shape
    head = pl.BlockSpec((rows, HD), lambda h: (0, h))
    return pl.pallas_call(
        attention_kernel,
        grid=(width // HD,),
        in_specs=[
            head,
            head,
            head,
            pl.BlockSpec((1, rows), lambda h: (0, 0)),
            pl.BlockSpec((rows, 1), lambda h: (0, 0)),
        ],
        out_specs=head,
        out_shape=jax.ShapeDtypeStruct((rows, width), jnp.bfloat16),
        compiler_params=pltpu.CompilerParams(vmem_limit_bytes=32 * 1024 * 1024),
        cost_estimate=COST,
    )(query, key, value, segment_ids.reshape(1, rows), segment_ids.reshape(rows, 1))


def projection_kernel(low_ref, heads_ref, weight_ref, theirs_ref, mine_ref):
    low = low_ref[0]
    pairs, _, rows, depth = heads_ref.shape
    theirs = heads_ref[:, 1 - low].reshape(pairs * rows, depth)
    theirs_ref[...] = (
        jnp.dot(theirs, weight_ref[...], preferred_element_type=jnp.float32)
        .astype(theirs_ref.dtype)
        .reshape(theirs_ref.shape)
    )
    mine = heads_ref[:, low].reshape(pairs * rows, depth)
    mine_ref[...] = jnp.dot(mine, weight_ref[...], preferred_element_type=jnp.float32).reshape(
        mine_ref.shape
    )


def projection(low, heads, weight, chunk, width):
    pairs, _, rows, depth = heads.shape
    tile = math.gcd(TILE, width)
    first = chunk * (width // tile)
    out = pl.BlockSpec((pairs, rows, tile), lambda i, low: (0, 0, i))
    return pl.pallas_call(
        projection_kernel,
        grid_spec=pltpu.PrefetchScalarGridSpec(
            num_scalar_prefetch=1,
            grid=(width // tile,),
            in_specs=[
                pl.BlockSpec(heads.shape, lambda i, low: (0, 0, 0, 0)),
                pl.BlockSpec((depth, tile), lambda i, low: (0, first + i)),
            ],
            out_specs=[out, out],
        ),
        out_shape=[
            jax.ShapeDtypeStruct((pairs, rows, width), jnp.bfloat16),
            jax.ShapeDtypeStruct((pairs, rows, width), jnp.float32),
        ],
        compiler_params=pltpu.CompilerParams(vmem_limit_bytes=32 * 1024 * 1024),
        cost_estimate=COST,
    )(low.reshape(1), heads, weight)


def pack_kernel(value_ref, packed_ref, scale_ref):
    wide = value_ref[...].astype(jnp.float32)
    scale = jnp.max(jnp.abs(wide), axis=1, keepdims=True) + 1e-06
    packed_ref[...] = (wide / scale).astype(packed_ref.dtype)
    scale_ref[...] = scale


def pack(value):
    rows, width = value.shape
    part = math.gcd(rows, 32)
    block = pl.BlockSpec((part, width), lambda i: (i, 0))
    return pl.pallas_call(
        pack_kernel,
        grid=(rows // part,),
        in_specs=[block],
        out_specs=[block, pl.BlockSpec((part, 1), lambda i: (i, 0))],
        out_shape=[
            jax.ShapeDtypeStruct(value.shape, value.dtype),
            jax.ShapeDtypeStruct((rows, 1), jnp.float32),
        ],
        compiler_params=pltpu.CompilerParams(vmem_limit_bytes=32 * 1024 * 1024),
        cost_estimate=pl.CostEstimate(flops=LATE, bytes_accessed=1000000, transcendentals=0),
    )(value)


def swap(value, axis, bit):
    count = lax.axis_size(axis)
    return lax.ppermute(value, axis, [(source, source ^ (1 << bit)) for source in range(count)])


def halve_kernel(own_ref, total_ref, arrived_ref, out_ref, kept_ref):
    own = own_ref[0]
    other = 1 - own
    out_ref[...] = (total_ref[:, other] + arrived_ref[:, other].astype(jnp.float32)).astype(
        out_ref.dtype
    )
    kept_ref[...] = total_ref[:, own] + arrived_ref[:, own].astype(jnp.float32)


def halve(own, total, arrived):
    groups, rows, width = total.shape
    tile = math.gcd(TILE, width)
    split = (groups // 2, 2, rows, width)
    whole = pl.BlockSpec(split[:3] + (tile,), lambda i, own: (0, 0, 0, i))
    half = pl.BlockSpec((groups // 2, rows, tile), lambda i, own: (0, 0, i))
    shape = (groups // 2, rows, width)
    return pl.pallas_call(
        halve_kernel,
        grid_spec=pltpu.PrefetchScalarGridSpec(
            num_scalar_prefetch=1,
            grid=(width // tile,),
            in_specs=[whole, whole],
            out_specs=[half, half],
        ),
        out_shape=[
            jax.ShapeDtypeStruct(shape, jnp.bfloat16),
            jax.ShapeDtypeStruct(shape, jnp.float32),
        ],
        compiler_params=pltpu.CompilerParams(vmem_limit_bytes=32 * 1024 * 1024),
        cost_estimate=COST,
    )(own.reshape(1), total.reshape(split), arrived.reshape(split))


def finish_kernel(count, *refs):
    input_ref, out_ref = refs[2 * count :]
    width = out_ref.shape[1] // count
    for chunk in range(count):
        columns = slice(chunk * width, (chunk + 1) * width)
        total = refs[chunk][...] + refs[count + chunk][...].astype(jnp.float32)
        out_ref[:, columns] = (input_ref[:, columns].astype(jnp.float32) + total).astype(
            out_ref.dtype
        )


def finish(totals, arrived, section_input):
    rows, width = section_input.shape
    count = len(totals)
    part = math.gcd(rows, 32)
    piece = pl.BlockSpec((part, width // count), lambda i: (i, 0))
    whole = pl.BlockSpec((part, width), lambda i: (i, 0))
    return pl.pallas_call(
        functools.partial(finish_kernel, count),
        grid=(rows // part,),
        in_specs=[piece] * (2 * count) + [whole],
        out_specs=whole,
        out_shape=jax.ShapeDtypeStruct(section_input.shape, section_input.dtype),
        compiler_params=pltpu.CompilerParams(vmem_limit_bytes=32 * 1024 * 1024),
        cost_estimate=COST,
    )(*totals, *arrived, section_input)


def scattered(theirs, total, axis):
    bits = lax.axis_size(axis).bit_length() - 1
    index = lax.axis_index(axis)
    arrived = swap(theirs, axis, 0)
    for bit in range(1, bits):
        out, total = halve((index >> bit) & 1, total, arrived)
        arrived = swap(out, axis, bit)
    return total[0], arrived[0]


def per_device(query_heads, key_heads, value_heads, segment_ids, section_input, out_weight):
    sections = lax.axis_size("pipe")
    tensors = lax.axis_size("tensor")
    mirrored = lax.ppermute(
        section_input, "pipe", [(source, sections - 1 - source) for source in range(sections)]
    )
    heads_out = attention(query_heads[0], key_heads[0], value_heads[0], segment_ids[0])
    rows, depth = heads_out.shape
    heads = heads_out.reshape(tensors // 2, 2, rows // tensors, depth)
    low = lax.axis_index("tensor") & 1
    width = out_weight.shape[2] // CHUNKS
    totals, arrived = [], []
    for chunk in range(CHUNKS):
        theirs, mine = projection(low, heads, out_weight[0], chunk, width)
        total, last = scattered(theirs, mine, "tensor")
        totals.append(total)
        arrived.append(last)
    section_out = finish(totals, arrived, section_input[0])
    received = lax.ppermute(
        section_out[None], "pipe", [(source, source + 1) for source in range(sections - 1)]
    )
    evicted, scale = pack(mirrored[0])
    return (received, evicted[None], scale.reshape(1, -1))


def solution(mesh):
    return jax.shard_map(
        per_device,
        mesh=mesh,
        in_specs=(
            P(("dp", "pipe"), None, "tensor"),
            P(("dp", "pipe"), None, "tensor"),
            P(("dp", "pipe"), None, "tensor"),
            P(("dp", "pipe"), None),
            P(("dp", "pipe"), "tensor", None),
            P(("dp", "pipe"), "tensor", None),
        ),
        out_specs=(
            P(("dp", "pipe"), "tensor", None),
            P(("dp", "pipe"), "tensor", None),
            P(("dp", "pipe"), "tensor"),
        ),
        check_vma=False,
    )
```

```python
import functools
import math

import jax
import jax.numpy as jnp
from jax import lax
from jax.experimental import pallas as pl
from jax.experimental.pallas import tpu as pltpu
from jax.sharding import PartitionSpec as P

HD = 128
CHUNKS = 4
TILE = 512
COST = pl.CostEstimate(flops=1000000, bytes_accessed=100000, transcendentals=0)
LATE = 40000000000
VMEM = 58 * 1024 * 1024
LAST = 16


def section_kernel(owners, chunks, low_ref, query_ref, key_ref, value_ref, ids_ref, weight_ref, *refs):
    theirs_refs, mine_refs = refs[:chunks], refs[chunks : 2 * chunks]
    heads_ref, held_ref, arrived = refs[2 * chunks :]
    step = pl.program_id(0)
    tile = held_ref.shape[2]

    def fetch(at):
        columns = pl.ds(pl.multiple_of(at * tile, tile), tile)
        return pltpu.make_async_copy(weight_ref.at[:, columns], held_ref.at[at], arrived.at[at])
    rows, depth = query_ref.shape
    part = rows // owners
    half = rows // 2
    tiles = pl.num_programs(0) // chunks

    @pl.when(step == 0)
    def _():
        for at in range(held_ref.shape[0]):
            fetch(at).start()
        query_ids = ids_ref[...].astype(jnp.float32)
        key_ids = jnp.transpose(jnp.broadcast_to(query_ids, (128, rows)))[:, :1]
        for begin in range(0, rows, half):
            end = begin + half
            key_at = lax.broadcasted_iota(jnp.int32, (end, half), 0)
            query_at = lax.broadcasted_iota(jnp.int32, (end, half), 1) + begin
            allowed = (key_ids[:end] == query_ids[:, begin:end]) & (key_at <= query_at)
            bias = jnp.where(allowed, 0.0, -1e30).astype(jnp.float32)
            for head in range(depth // HD):
                lanes = slice(head * HD, (head + 1) * HD)
                scores = lax.dot_general(
                    key_ref[:end, lanes],
                    query_ref[begin:end, lanes],
                    (((1,), (1,)), ((), ())),
                    preferred_element_type=jnp.float32,
                )
                scores = scores * (math.log2(math.e) / math.sqrt(HD)) + bias
                expons = jnp.exp2(scores - jnp.max(scores, axis=0, keepdims=True))
                weights = expons * (1.0 / jnp.sum(expons, axis=0, keepdims=True))
                out = lax.dot_general(
                    value_ref[:end, lanes],
                    weights.astype(jnp.bfloat16),
                    (((0,), (0,)), ((), ())),
                    preferred_element_type=jnp.float32,
                )
                out = jnp.transpose(out).astype(jnp.bfloat16)
                for owner in range(begin // part, end // part):
                    place = jnp.where(low_ref[0] == owner % 2, half, 0) + owner // 2 * part
                    heads_ref[pl.ds(pl.multiple_of(place, part), part), lanes] = out[
                        owner * part - begin : (owner + 1) * part - begin
                    ]

    fetch(step).wait()
    product = jnp.dot(heads_ref[...], held_ref[step], preferred_element_type=jnp.float32)
    for chunk in range(chunks):

        @pl.when(step // tiles == chunk)
        def _(chunk=chunk):
            theirs, mine = theirs_refs[chunk], mine_refs[chunk]
            theirs[...] = product[:half].astype(theirs.dtype).reshape(theirs.shape)
            mine[...] = product[half:].reshape(mine.shape)


def section(owners, low, query, key, value, segment_ids, weight):
    rows, depth = query.shape
    columns = weight.shape[1]
    width = columns // CHUNKS
    tile = math.gcd(TILE, width)
    tiles = width // tile
    shape = (owners // 2, rows // owners, width)
    full = lambda array: pl.BlockSpec(array.shape, lambda i, low: (0, 0))

    def piece(chunk):
        return pl.BlockSpec(
            shape[:2] + (tile,), lambda i, low: (0, 0, jnp.clip(i - chunk * tiles, 0, tiles - 1))
        )

    ids = segment_ids.reshape(1, rows)
    out = pl.pallas_call(
        functools.partial(section_kernel, owners, CHUNKS),
        grid_spec=pltpu.PrefetchScalarGridSpec(
            num_scalar_prefetch=1,
            grid=(columns // tile,),
            in_specs=[
                full(query),
                full(key),
                full(value),
                full(ids),
                pl.BlockSpec(memory_space=pl.ANY),
            ],
            out_specs=[piece(chunk) for chunk in range(CHUNKS)] * 2,
            scratch_shapes=[
                pltpu.VMEM((rows, depth), jnp.bfloat16),
                pltpu.VMEM((columns // tile, depth, tile), jnp.bfloat16),
                pltpu.SemaphoreType.DMA((columns // tile,)),
            ],
        ),
        out_shape=[jax.ShapeDtypeStruct(shape, jnp.bfloat16)] * CHUNKS
        + [jax.ShapeDtypeStruct(shape, jnp.float32)] * CHUNKS,
        compiler_params=pltpu.CompilerParams(vmem_limit_bytes=VMEM),
        cost_estimate=COST,
    )(low.reshape(1), query, key, value, ids, weight)
    return out[:CHUNKS], out[CHUNKS:]


def pack_kernel(value_ref, packed_ref, scale_ref):
    wide = value_ref[...].astype(jnp.float32)
    scale = jnp.max(jnp.abs(wide), axis=1, keepdims=True) + 1e-06
    packed_ref[...] = (wide / scale).astype(packed_ref.dtype)
    scale_ref[...] = scale


def pack(value):
    rows, width = value.shape
    part = math.gcd(rows, 32)
    block = pl.BlockSpec((part, width), lambda i: (i, 0))
    return pl.pallas_call(
        pack_kernel,
        grid=(rows // part,),
        in_specs=[block],
        out_specs=[block, pl.BlockSpec((part, 1), lambda i: (i, 0))],
        out_shape=[
            jax.ShapeDtypeStruct(value.shape, value.dtype),
            jax.ShapeDtypeStruct((rows, 1), jnp.float32),
        ],
        compiler_params=pltpu.CompilerParams(vmem_limit_bytes=61 * 1024 * 1024),
        cost_estimate=pl.CostEstimate(flops=LATE, bytes_accessed=1000000, transcendentals=0),
    )(value)


def swap(value, axis, bit):
    count = lax.axis_size(axis)
    return lax.ppermute(value, axis, [(source, source ^ (1 << bit)) for source in range(count)])


def halve_kernel(own_ref, total_ref, arrived_ref, out_ref, kept_ref):
    own = own_ref[0]
    other = 1 - own
    out_ref[...] = (total_ref[:, other] + arrived_ref[:, other].astype(jnp.float32)).astype(
        out_ref.dtype
    )
    kept_ref[...] = total_ref[:, own] + arrived_ref[:, own].astype(jnp.float32)


def halve(own, total, arrived):
    groups, rows, width = total.shape
    tile = math.gcd(TILE, width)
    split = (groups // 2, 2, rows, width)
    whole = pl.BlockSpec(split[:3] + (tile,), lambda i, own: (0, 0, 0, i))
    half = pl.BlockSpec((groups // 2, rows, tile), lambda i, own: (0, 0, i))
    shape = (groups // 2, rows, width)
    return pl.pallas_call(
        halve_kernel,
        grid_spec=pltpu.PrefetchScalarGridSpec(
            num_scalar_prefetch=1,
            grid=(width // tile,),
            in_specs=[whole, whole],
            out_specs=[half, half],
        ),
        out_shape=[
            jax.ShapeDtypeStruct(shape, jnp.bfloat16),
            jax.ShapeDtypeStruct(shape, jnp.float32),
        ],
        compiler_params=pltpu.CompilerParams(vmem_limit_bytes=16 * 1024 * 1024),
        cost_estimate=COST,
    )(own.reshape(1), total.reshape(split), arrived.reshape(split))


def finish_kernel(count, *refs):
    input_ref, *out_refs = refs[2 * count :]
    width = input_ref.shape[1] // count

    def write(out_ref):
        for chunk in range(count):
            columns = slice(chunk * width, (chunk + 1) * width)
            total = refs[chunk][...] + refs[count + chunk][...].astype(jnp.float32)
            out_ref[:, columns] = (input_ref[:, columns].astype(jnp.float32) + total).astype(
                out_ref.dtype
            )

    is_last = pl.program_id(0) == pl.num_programs(0) - 1
    pl.when(jnp.logical_not(is_last))(lambda: write(out_refs[0]))
    pl.when(is_last)(lambda: write(out_refs[1]))


def finish(totals, arrived, section_input):
    rows, width = section_input.shape
    count = len(totals)
    part = math.gcd(rows // 2, LAST)
    piece = pl.BlockSpec((part, width // count), lambda i: (i, 0))
    whole = pl.BlockSpec((part, width), lambda i: (i, 0))
    steps = rows // part
    return pl.pallas_call(
        functools.partial(finish_kernel, count),
        grid=(steps,),
        in_specs=[piece] * (2 * count) + [whole],
        out_specs=[
            pl.BlockSpec((part, width), lambda i: (jnp.minimum(i, steps - 2), 0)),
            pl.BlockSpec((part, width), lambda i: (0, 0)),
        ],
        out_shape=[
            jax.ShapeDtypeStruct((rows - part, width), section_input.dtype),
            jax.ShapeDtypeStruct((part, width), section_input.dtype),
        ],
        compiler_params=pltpu.CompilerParams(vmem_limit_bytes=16 * 1024 * 1024),
        cost_estimate=COST,
    )(*totals, *arrived, section_input)


def place_kernel(first, part_ref, *refs):
    out_ref, sent = refs[-2:]
    rows = part_ref.shape[0]
    copy = pltpu.make_async_copy(part_ref, out_ref.at[pl.ds(first, rows)], sent)
    copy.start()
    copy.wait()


def place(part, first, rows, into=None):
    anywhere = pl.BlockSpec(memory_space=pl.ANY)
    operands = (part,) if into is None else (part, into)
    return pl.pallas_call(
        functools.partial(place_kernel, first),
        in_specs=[anywhere] * len(operands),
        out_specs=anywhere,
        out_shape=jax.ShapeDtypeStruct((rows, part.shape[1]), part.dtype),
        input_output_aliases={} if into is None else {1: 0},
        scratch_shapes=[pltpu.SemaphoreType.DMA],
        compiler_params=pltpu.CompilerParams(vmem_limit_bytes=16 * 1024 * 1024),
        cost_estimate=COST,
    )(*operands)


def scattered(theirs, total, axis):
    bits = lax.axis_size(axis).bit_length() - 1
    index = lax.axis_index(axis)
    arrived = swap(theirs, axis, 0)
    for bit in range(1, bits):
        out, total = halve((index >> bit) & 1, total, arrived)
        arrived = swap(out, axis, bit)
    return total[0], arrived[0]


def per_device(query_heads, key_heads, value_heads, segment_ids, section_input, out_weight):
    sections = lax.axis_size("pipe")
    tensors = lax.axis_size("tensor")
    mirrored = lax.ppermute(
        section_input, "pipe", [(source, sections - 1 - source) for source in range(sections)]
    )
    theirs, mine = section(
        tensors,
        lax.axis_index("tensor") & 1,
        query_heads[0],
        key_heads[0],
        value_heads[0],
        segment_ids[0],
        out_weight[0],
    )
    pairs = [scattered(*parts, "tensor") for parts in zip(theirs, mine)]
    totals, arrived = zip(*pairs)
    onward = [
        lax.ppermute(part, "pipe", [(source, source + 1) for source in range(sections - 1)])
        for part in finish(totals, arrived, section_input[0])
    ]
    received = place(onward[0], 0, section_input.shape[1])
    received = place(onward[1], onward[0].shape[0], section_input.shape[1], received)[None]
    evicted, scale = pack(mirrored[0])
    return (received, evicted[None], scale.reshape(1, -1))


def solution(mesh):
    return jax.shard_map(
        per_device,
        mesh=mesh,
        in_specs=(
            P(("dp", "pipe"), None, "tensor"),
            P(("dp", "pipe"), None, "tensor"),
            P(("dp", "pipe"), None, "tensor"),
            P(("dp", "pipe"), None),
            P(("dp", "pipe"), "tensor", None),
            P(("dp", "pipe"), "tensor", None),
        ),
        out_specs=(
            P(("dp", "pipe"), "tensor", None),
            P(("dp", "pipe"), "tensor", None),
            P(("dp", "pipe"), "tensor"),
        ),
        check_vma=False,
    )
```

```python
import functools
import math

import jax
import jax.numpy as jnp
from jax import lax
from jax.experimental import pallas as pl
from jax.experimental.pallas import tpu as pltpu
from jax.sharding import PartitionSpec as P

HD = 128
CHUNKS = 4
TILE = 512
COST = pl.CostEstimate(flops=1000000, bytes_accessed=100000, transcendentals=0)
LATE = 40000000000
VMEM = 58 * 1024 * 1024
LAST = 16


def section_kernel(owners, chunks, low_ref, query_ref, key_ref, value_ref, ids_ref, weight_ref, *refs):
    theirs_refs, mine_refs = refs[:chunks], refs[chunks : 2 * chunks]
    heads_ref, held_ref, arrived = refs[2 * chunks :]
    step = pl.program_id(0)
    tile = held_ref.shape[2]

    def fetch(at):
        columns = pl.ds(pl.multiple_of(at * tile, tile), tile)
        return pltpu.make_async_copy(weight_ref.at[:, columns], held_ref.at[at], arrived.at[at])
    rows, depth = query_ref.shape
    part = rows // owners
    half = rows // 2
    tiles = pl.num_programs(0) // chunks

    @pl.when(step == 0)
    def _():
        for at in range(held_ref.shape[0]):
            fetch(at).start()
        query_ids = ids_ref[...].astype(jnp.float32)
        key_ids = jnp.transpose(jnp.broadcast_to(query_ids, (128, rows)))[:, :1]
        for begin in range(0, rows, half):
            end = begin + half
            key_at = lax.broadcasted_iota(jnp.int32, (end, half), 0)
            query_at = lax.broadcasted_iota(jnp.int32, (end, half), 1) + begin
            allowed = (key_ids[:end] == query_ids[:, begin:end]) & (key_at <= query_at)
            bias = jnp.where(allowed, 0.0, -1e30).astype(jnp.float32)

            def one_head(head, carry, begin=begin, end=end, bias=bias):
                lanes = pl.ds(pl.multiple_of(head * HD, HD), HD)
                scores = lax.dot_general(
                    key_ref[:end, lanes],
                    query_ref[begin:end, lanes],
                    (((1,), (1,)), ((), ())),
                    preferred_element_type=jnp.float32,
                )
                scores = scores * (math.log2(math.e) / math.sqrt(HD)) + bias
                expons = jnp.exp2(scores - jnp.max(scores, axis=0, keepdims=True))
                weights = expons * (1.0 / jnp.sum(expons, axis=0, keepdims=True))
                out = lax.dot_general(
                    value_ref[:end, lanes],
                    weights.astype(jnp.bfloat16),
                    (((0,), (0,)), ((), ())),
                    preferred_element_type=jnp.float32,
                )
                out = jnp.transpose(out).astype(jnp.bfloat16)
                for owner in range(begin // part, end // part):
                    place = jnp.where(low_ref[0] == owner % 2, half, 0) + owner // 2 * part
                    heads_ref[pl.ds(pl.multiple_of(place, part), part), lanes] = out[
                        owner * part - begin : (owner + 1) * part - begin
                    ]
                return carry

            lax.fori_loop(0, depth // HD, one_head, 0)

    fetch(step).wait()
    product = jnp.dot(heads_ref[...], held_ref[step], preferred_element_type=jnp.float32)
    for chunk in range(chunks):

        @pl.when(step // tiles == chunk)
        def _(chunk=chunk):
            theirs, mine = theirs_refs[chunk], mine_refs[chunk]
            theirs[...] = product[:half].astype(theirs.dtype).reshape(theirs.shape)
            mine[...] = product[half:].reshape(mine.shape)


def section(owners, low, query, key, value, segment_ids, weight):
    rows, depth = query.shape
    columns = weight.shape[1]
    width = columns // CHUNKS
    tile = math.gcd(TILE, width)
    tiles = width // tile
    shape = (owners // 2, rows // owners, width)
    full = lambda array: pl.BlockSpec(array.shape, lambda i, low: (0, 0))

    def piece(chunk):
        return pl.BlockSpec(
            shape[:2] + (tile,), lambda i, low: (0, 0, jnp.clip(i - chunk * tiles, 0, tiles - 1))
        )

    ids = segment_ids.reshape(1, rows)
    out = pl.pallas_call(
        functools.partial(section_kernel, owners, CHUNKS),
        grid_spec=pltpu.PrefetchScalarGridSpec(
            num_scalar_prefetch=1,
            grid=(columns // tile,),
            in_specs=[
                full(query),
                full(key),
                full(value),
                full(ids),
                pl.BlockSpec(memory_space=pl.ANY),
            ],
            out_specs=[piece(chunk) for chunk in range(CHUNKS)] * 2,
            scratch_shapes=[
                pltpu.VMEM((rows, depth), jnp.bfloat16),
                pltpu.VMEM((columns // tile, depth, tile), jnp.bfloat16),
                pltpu.SemaphoreType.DMA((columns // tile,)),
            ],
        ),
        out_shape=[jax.ShapeDtypeStruct(shape, jnp.bfloat16)] * CHUNKS
        + [jax.ShapeDtypeStruct(shape, jnp.float32)] * CHUNKS,
        compiler_params=pltpu.CompilerParams(vmem_limit_bytes=VMEM),
        cost_estimate=COST,
    )(low.reshape(1), query, key, value, ids, weight)
    return out[:CHUNKS], out[CHUNKS:]


def pack_kernel(value_ref, packed_ref, scale_ref):
    wide = value_ref[...].astype(jnp.float32)
    scale = jnp.max(jnp.abs(wide), axis=1, keepdims=True) + 1e-06
    packed_ref[...] = (wide / scale).astype(packed_ref.dtype)
    scale_ref[...] = scale


def pack(value):
    rows, width = value.shape
    part = math.gcd(rows, 32)
    block = pl.BlockSpec((part, width), lambda i: (i, 0))
    return pl.pallas_call(
        pack_kernel,
        grid=(rows // part,),
        in_specs=[block],
        out_specs=[block, pl.BlockSpec((part, 1), lambda i: (i, 0))],
        out_shape=[
            jax.ShapeDtypeStruct(value.shape, value.dtype),
            jax.ShapeDtypeStruct((rows, 1), jnp.float32),
        ],
        compiler_params=pltpu.CompilerParams(vmem_limit_bytes=61 * 1024 * 1024),
        cost_estimate=pl.CostEstimate(flops=LATE, bytes_accessed=1000000, transcendentals=0),
    )(value)


def swap(value, axis, bit):
    count = lax.axis_size(axis)
    return lax.ppermute(value, axis, [(source, source ^ (1 << bit)) for source in range(count)])


def halve_kernel(own_ref, total_ref, arrived_ref, out_ref, kept_ref):
    own = own_ref[0]
    other = 1 - own
    out_ref[...] = (total_ref[:, other] + arrived_ref[:, other].astype(jnp.float32)).astype(
        out_ref.dtype
    )
    kept_ref[...] = total_ref[:, own] + arrived_ref[:, own].astype(jnp.float32)


def halve(own, total, arrived):
    groups, rows, width = total.shape
    tile = math.gcd(TILE, width)
    split = (groups // 2, 2, rows, width)
    whole = pl.BlockSpec(split[:3] + (tile,), lambda i, own: (0, 0, 0, i))
    half = pl.BlockSpec((groups // 2, rows, tile), lambda i, own: (0, 0, i))
    shape = (groups // 2, rows, width)
    return pl.pallas_call(
        halve_kernel,
        grid_spec=pltpu.PrefetchScalarGridSpec(
            num_scalar_prefetch=1,
            grid=(width // tile,),
            in_specs=[whole, whole],
            out_specs=[half, half],
        ),
        out_shape=[
            jax.ShapeDtypeStruct(shape, jnp.bfloat16),
            jax.ShapeDtypeStruct(shape, jnp.float32),
        ],
        compiler_params=pltpu.CompilerParams(vmem_limit_bytes=16 * 1024 * 1024),
        cost_estimate=COST,
    )(own.reshape(1), total.reshape(split), arrived.reshape(split))


def finish_kernel(count, *refs):
    input_ref, *out_refs = refs[2 * count :]
    width = input_ref.shape[1] // count

    def write(out_ref):
        for chunk in range(count):
            columns = slice(chunk * width, (chunk + 1) * width)
            total = refs[chunk][...] + refs[count + chunk][...].astype(jnp.float32)
            out_ref[:, columns] = (input_ref[:, columns].astype(jnp.float32) + total).astype(
                out_ref.dtype
            )

    is_last = pl.program_id(0) == pl.num_programs(0) - 1
    pl.when(jnp.logical_not(is_last))(lambda: write(out_refs[0]))
    pl.when(is_last)(lambda: write(out_refs[1]))


def finish(totals, arrived, section_input):
    rows, width = section_input.shape
    count = len(totals)
    part = math.gcd(rows // 2, LAST)
    piece = pl.BlockSpec((part, width // count), lambda i: (i, 0))
    whole = pl.BlockSpec((part, width), lambda i: (i, 0))
    steps = rows // part
    return pl.pallas_call(
        functools.partial(finish_kernel, count),
        grid=(steps,),
        in_specs=[piece] * (2 * count) + [whole],
        out_specs=[
            pl.BlockSpec((part, width), lambda i: (jnp.minimum(i, steps - 2), 0)),
            pl.BlockSpec((part, width), lambda i: (0, 0)),
        ],
        out_shape=[
            jax.ShapeDtypeStruct((rows - part, width), section_input.dtype),
            jax.ShapeDtypeStruct((part, width), section_input.dtype),
        ],
        compiler_params=pltpu.CompilerParams(vmem_limit_bytes=16 * 1024 * 1024),
        cost_estimate=COST,
    )(*totals, *arrived, section_input)


def place_kernel(part_ref, out_ref, sent):
    copy = pltpu.make_async_copy(part_ref, out_ref.at[: part_ref.shape[0]], sent)
    copy.start()
    copy.wait()


def place(part, rows):
    anywhere = pl.BlockSpec(memory_space=pl.ANY)
    return pl.pallas_call(
        place_kernel,
        in_specs=[anywhere],
        out_specs=anywhere,
        out_shape=jax.ShapeDtypeStruct((rows, part.shape[1]), part.dtype),
        scratch_shapes=[pltpu.SemaphoreType.DMA],
        compiler_params=pltpu.CompilerParams(vmem_limit_bytes=16 * 1024 * 1024),
        cost_estimate=COST,
    )(part)


def scattered(theirs, total, axis):
    bits = lax.axis_size(axis).bit_length() - 1
    index = lax.axis_index(axis)
    arrived = swap(theirs, axis, 0)
    for bit in range(1, bits):
        out, total = halve((index >> bit) & 1, total, arrived)
        arrived = swap(out, axis, bit)
    return total[0], arrived[0]


def per_device(query_heads, key_heads, value_heads, segment_ids, section_input, out_weight):
    sections = lax.axis_size("pipe")
    tensors = lax.axis_size("tensor")
    mirrored = lax.ppermute(
        section_input, "pipe", [(source, sections - 1 - source) for source in range(sections)]
    )
    theirs, mine = section(
        tensors,
        lax.axis_index("tensor") & 1,
        query_heads[0],
        key_heads[0],
        value_heads[0],
        segment_ids[0],
        out_weight[0],
    )
    pairs = [scattered(*parts, "tensor") for parts in zip(theirs, mine)]
    totals, arrived = zip(*pairs)
    onward = [
        lax.ppermute(part, "pipe", [(source, source + 1) for source in range(sections - 1)])
        for part in finish(totals, arrived, section_input[0])
    ]
    received = place(onward[0], section_input.shape[1])
    received = lax.dynamic_update_slice(received, onward[1], (onward[0].shape[0], 0))[None]
    evicted, scale = pack(mirrored[0])
    return (received, evicted[None], scale.reshape(1, -1))


def solution(mesh):
    return jax.shard_map(
        per_device,
        mesh=mesh,
        in_specs=(
            P(("dp", "pipe"), None, "tensor"),
            P(("dp", "pipe"), None, "tensor"),
            P(("dp", "pipe"), None, "tensor"),
            P(("dp", "pipe"), None),
            P(("dp", "pipe"), "tensor", None),
            P(("dp", "pipe"), "tensor", None),
        ),
        out_specs=(
            P(("dp", "pipe"), "tensor", None),
            P(("dp", "pipe"), "tensor", None),
            P(("dp", "pipe"), "tensor"),
        ),
        check_vma=False,
    )
```
